1024 devices in a mesh: grp: 16 (over z, core), blk: 64 (over y, x).
Axes of the slice: x: 8, y: 8, z: 8, core: 2. Of those that a mesh axis runs over, the one named last changes fastest.
Arguments:
- features: bfloat16 [1048576, 128], P(('grp', 'blk')), may hold values from -6 to 6
- cotangent: bfloat16 [1048576, 256], P(('grp', 'blk')), may hold values from -15 to 15
- self_weight: bfloat16 [128, 256], replicated, may hold values from -0.5 to 0.5
- mean_weight: bfloat16 [128, 256], replicated, may hold values from -0.5 to 0.5
- bias_term: float32 [256], replicated, may hold values from -3 to 3
- edge_source: int32 [16, 64, 64, 128], P('grp', 'blk'), may hold values from 0 to 1023
- edge_target: int32 [16, 64, 64, 128], P('grp', 'blk'), may hold values from 0 to 3071
- block_counts: int32 [16, 64], P('grp', 'blk'), may hold values from 1 to 64
- receive_rows: int32 [16, 64, 16, 128], P('grp', 'blk'), may hold values from 0 to 1007
Outputs:
- activation: bfloat16 [1048576, 256], P(('grp', 'blk'))
- feature_grad: bfloat16 [1048576, 128], P(('grp', 'blk'))
- self_grad: float32 [128, 256], replicated
- mean_grad: float32 [128, 256], replicated
- bias_grad: float32 [256], replicated
The draws below stay inside these ranges and needn't reach their ends.
All inputs are finite; a program needn't handle non-finite values.
Results may differ from the reference program's by a relative error of at most 0.0055.
Values may be sent and summed in bfloat16 or wider, within the bound.
A program may use at most 32 MiB of HBM per device.

```python
import jax
import jax.numpy as jnp
from jax import lax

F = 128
H = 256
V_DEV = 1024
HUB_DEV = 16
CAP = 128
MAXB = 64
BLOCK = 128
VERTS = 1048576
N_GRP = 16
N_BLK = 64


def draw_edge_target(key, part):
    key = jax.random.fold_in(key, 11)
    first, second, third, fourth, fifth = jax.random.split(key, 5)
    shape = (N_GRP, N_BLK, MAXB, BLOCK)
    slot_count = N_GRP * CAP
    hub_count = HUB_DEV * N_BLK
    regular = jax.random.randint(first, shape, 0, slot_count)
    spread = jax.random.randint(second, shape, 0, hub_count)
    ranked = spread * spread // hub_count * spread // hub_count
    hub_order = jax.random.permutation(fifth, hub_count).astype(jnp.int32)
    hubward = slot_count + hub_order[ranked]
    picked = jax.random.randint(third, shape, 0, 4) == 0
    target = jnp.where(picked, hubward, regular).reshape(-1)
    spots = jax.random.randint(fourth, (2,), 0, target.shape[0] // 2)
    target = target.at[2 * spots[0]].set(0)
    target = target.at[2 * spots[1] + 1].set(slot_count + hub_count - 1)
    return target.reshape(shape).astype(jnp.int32)


def draw_block_counts(key, part):
    key = jax.random.fold_in(key, 12)
    first, second, third, fourth, fifth = jax.random.split(key, 5)
    shape = (N_GRP, N_BLK)
    lower = jax.random.randint(first, shape, MAXB // 4, 3 * MAXB // 4 + 1)
    higher = jax.random.randint(second, shape, 3 * MAXB // 4, MAXB + 1)
    heavy = jax.random.randint(third, shape, 0, 8) == 0
    counts_all = jnp.where(heavy, higher, lower).reshape(-1)
    total_devices = counts_all.shape[0]
    full_spot = jax.random.randint(fourth, (), 0, total_devices)
    step_spot = jax.random.randint(fifth, (), 0, total_devices - 1)
    counts_all = counts_all.at[full_spot].set(MAXB)
    counts_all = counts_all.at[(full_spot + 1 + step_spot) % total_devices].set(1)
    return counts_all.reshape(shape).astype(jnp.int32)


def draw_cotangent(key, part):
    key = jax.random.fold_in(key, 13)
    row_of = jnp.arange(VERTS, dtype=jnp.int32) % V_DEV
    is_hub = row_of >= V_DEV - HUB_DEV
    base = jax.random.normal(key, (VERTS, H), jnp.float32)
    scale = jnp.where(is_hub, 5.0, 1.0)
    return jnp.clip(base * scale[:, None], -15.0, 15.0).astype(jnp.bfloat16)


def plant(array, key, low, top_value):
    shape = array.shape
    spot = [jax.random.randint(jax.random.fold_in(key, axis), (), 0, shape[axis]) for axis in range(len(shape))]
    array = array.at[tuple(spot)].set(low)
    longest = shape.index(max(shape))
    spot[longest] = (spot[longest] + 1) % shape[longest]
    return array.at[tuple(spot)].set(top_value)


def block_scale(stream_key, dims, shards, smallest, top_value):
    level = 1.0
    for axis_at, shards_of in shards:
        draws = jax.random.uniform(jax.random.fold_in(jax.random.fold_in(stream_key, 6), axis_at), (shards_of,), jnp.float32, smallest / len(shards), top_value / len(shards))
        level = level * jnp.repeat(jnp.exp(draws), dims[axis_at] // shards_of).reshape((-1,) + (1,) * (len(dims) - 1 - axis_at))
    return level


def bell_draw(stream_key, extent, scale, limit, shards=(), held_as=jnp.bfloat16):
    entries = scale * jax.random.normal(stream_key, extent, jnp.float32)
    if shards:
        entries = entries * block_scale(stream_key, extent, shards, -0.22, 0.18)
    return jnp.clip(entries, -limit, limit).astype(held_as)


def setup_inputs(seed: int = 0) -> dict:
    streams_of = jax.random.split(jax.random.key(seed), 10)
    return {
        "features": bell_draw(streams_of[0], (VERTS, F), 1.0, 6.0, ((0, 1024),)),
        "cotangent": draw_cotangent(jax.random.fold_in(streams_of[9], 71), 0),
        "self_weight": bell_draw(streams_of[2], (F, H), F ** -0.5, 0.5),
        "mean_weight": bell_draw(streams_of[3], (F, H), F ** -0.5, 0.5),
        "bias_term": bell_draw(streams_of[4], (H,), 0.5, 3.0, (), jnp.float32),
        "edge_source": plant(jax.random.randint(streams_of[5], (N_GRP, N_BLK, MAXB, BLOCK), 0, V_DEV), jax.random.fold_in(streams_of[5], 1), 0, V_DEV - 1).astype(jnp.int32),
        "edge_target": draw_edge_target(jax.random.fold_in(streams_of[9], 71), 0),
        "block_counts": draw_block_counts(jax.random.fold_in(streams_of[9], 71), 0),
        "receive_rows": plant(jax.random.randint(streams_of[8], (N_GRP, N_BLK, N_GRP, CAP), 0, V_DEV - HUB_DEV), jax.random.fold_in(streams_of[8], 1), 0, (V_DEV - HUB_DEV) - 1).astype(jnp.int32),
    }


def layer_pass(inputs, neighbour_mean, upstream, self_weight, mean_weight, bias_term):
    pre_act = jnp.dot(inputs, self_weight, preferred_element_type=jnp.float32) + jnp.dot(neighbour_mean, mean_weight, preferred_element_type=jnp.float32) + bias_term
    sigmoid_part = jax.nn.sigmoid(pre_act)
    activation = (pre_act * sigmoid_part).astype(jnp.bfloat16)
    pre_grad = (upstream.astype(jnp.float32) * sigmoid_part * (1.0 + pre_act * (1.0 - sigmoid_part))).astype(jnp.bfloat16)
    return activation, pre_grad


def device_totals(source_table, take_index, put_index, live_blocks, buckets):
    usable = jnp.arange(take_index.shape[0], dtype=jnp.int32)[:, None] < live_blocks
    usable = jnp.broadcast_to(usable, take_index.shape).reshape(-1)
    target = jnp.where(usable, put_index.reshape(-1), buckets)
    totals = jax.ops.segment_sum(source_table[take_index.reshape(-1)].astype(jnp.float32), target, buckets + 1)
    tallies = jax.ops.segment_sum(usable.astype(jnp.float32), target, buckets + 1)
    return totals[:buckets], tallies[:buckets]


def segment_rows(values_in, row_list):
    return jax.ops.segment_sum(values_in, row_list, V_DEV - HUB_DEV)


def pick_rows(row_table, row_list):
    return row_table[row_list]


def reference(features, cotangent, self_weight, mean_weight, bias_term, edge_source, edge_target, block_counts, receive_rows):
    slot_count = N_GRP * CAP
    hub_count = HUB_DEV * N_BLK
    bucket_count = slot_count + hub_count
    regular = V_DEV - HUB_DEV
    inputs = features.reshape(N_GRP, N_BLK, V_DEV, F)
    upstream = cotangent.reshape(N_GRP, N_BLK, V_DEV, H)

    def forward_totals(table, take_index, put_index, live_blocks):
        return device_totals(table, take_index, put_index, live_blocks, bucket_count)

    def backward_totals(table, take_index, put_index, live_blocks):
        return device_totals(table, take_index, put_index, live_blocks, V_DEV)

    group_forward = jax.vmap(forward_totals)
    group_backward = jax.vmap(backward_totals)

    def hub_pass(carry, blk_index):
        totals, tallies = group_forward(inputs[:, blk_index], edge_source[:, blk_index], edge_target[:, blk_index], block_counts[:, blk_index])
        return (carry[0] + totals[:, slot_count:], carry[1] + tallies[:, slot_count:]), None

    hub_zero = (jnp.zeros((N_GRP, hub_count, F), jnp.float32), jnp.zeros((N_GRP, hub_count), jnp.float32))
    (hub_sums, hub_degree), unused = lax.scan(hub_pass, hub_zero, jnp.arange(N_BLK, dtype=jnp.int32))
    hub_divisor = jnp.maximum(hub_degree, 1.0)[:, :, None]
    hub_mean = (hub_sums / hub_divisor).astype(jnp.bfloat16)
    hub_inputs = inputs[:, :, regular:].reshape(N_GRP * hub_count, F)
    hub_upstream = upstream[:, :, regular:].reshape(N_GRP * hub_count, H)
    unused_act, hub_pre = layer_pass(hub_inputs, hub_mean.reshape(-1, F), hub_upstream, self_weight, mean_weight, bias_term)
    hub_back = (jnp.dot(hub_pre, mean_weight.T, preferred_element_type=jnp.float32).reshape(N_GRP, hub_count, F) / hub_divisor).astype(jnp.bfloat16)

    def main_pass(carry, blk_index):
        block_inputs = inputs[:, blk_index]
        sources = edge_source[:, blk_index]
        targets = edge_target[:, blk_index]
        counts_here = block_counts[:, blk_index]
        totals, tallies = group_forward(block_inputs, sources, targets, counts_here)
        partials = totals[:, :slot_count].astype(jnp.bfloat16).reshape(N_GRP, N_GRP, CAP, F)
        slot_tally = tallies[:, :slot_count].astype(jnp.bfloat16).reshape(N_GRP, N_GRP, CAP)
        arrived = jnp.transpose(partials, (1, 0, 2, 3)).reshape(N_GRP, slot_count, F)
        arrived_tally = jnp.transpose(slot_tally, (1, 0, 2)).reshape(N_GRP, slot_count)
        row_index = receive_rows[:, blk_index].reshape(N_GRP, slot_count)
        summed = jax.vmap(segment_rows)(arrived.astype(jnp.float32), row_index)
        degree = jax.vmap(segment_rows)(arrived_tally.astype(jnp.float32), row_index)
        own_sums = lax.dynamic_slice_in_dim(hub_sums, blk_index * HUB_DEV, HUB_DEV, 1)
        own_degree = lax.dynamic_slice_in_dim(hub_degree, blk_index * HUB_DEV, HUB_DEV, 1)
        summed = jnp.concatenate([summed, own_sums], 1)
        degree = jnp.concatenate([degree, own_degree], 1)
        divisor = jnp.maximum(degree, 1.0)[:, :, None]
        neighbour_mean = (summed / divisor).astype(jnp.bfloat16)
        flat_inputs = block_inputs.reshape(-1, F)
        flat_mean = neighbour_mean.reshape(-1, F)
        activation, pre_grad = layer_pass(flat_inputs, flat_mean, upstream[:, blk_index].reshape(-1, H), self_weight, mean_weight, bias_term)
        self_part = jnp.dot(flat_inputs.T, pre_grad, preferred_element_type=jnp.float32)
        mean_part = jnp.dot(flat_mean.T, pre_grad, preferred_element_type=jnp.float32)
        bias_part = jnp.sum(pre_grad.astype(jnp.float32), 0)
        mean_rows = (jnp.dot(pre_grad, mean_weight.T, preferred_element_type=jnp.float32).reshape(N_GRP, V_DEV, F) / divisor).astype(jnp.bfloat16)
        going_back = jax.vmap(pick_rows)(mean_rows, row_index).reshape(N_GRP, N_GRP, CAP, F)
        going_back = jnp.transpose(going_back, (1, 0, 2, 3)).reshape(N_GRP, slot_count, F)
        grad_table = jnp.concatenate([going_back, hub_back], 1)
        edge_grads, unused_tally = group_backward(grad_table, targets, sources, counts_here)
        own_grad = jnp.dot(pre_grad, self_weight.T, preferred_element_type=jnp.float32).reshape(N_GRP, V_DEV, F)
        feature_grad = (own_grad + edge_grads).astype(jnp.bfloat16)
        carry = (carry[0] + self_part, carry[1] + mean_part, carry[2] + bias_part)
        return carry, (activation.reshape(N_GRP, V_DEV, H), feature_grad)

    grad_zero = (jnp.zeros((F, H), jnp.float32), jnp.zeros((F, H), jnp.float32), jnp.zeros((H,), jnp.float32))
    (self_grad, mean_grad, bias_grad), (activation, feature_grad) = lax.scan(main_pass, grad_zero, jnp.arange(N_BLK, dtype=jnp.int32))
    activation = jnp.transpose(activation, (1, 0, 2, 3)).reshape(N_GRP * N_BLK * V_DEV, H)
    feature_grad = jnp.transpose(feature_grad, (1, 0, 2, 3)).reshape(N_GRP * N_BLK * V_DEV, F)
    return (activation, feature_grad, self_grad, mean_grad, bias_grad)
```

```python
import jax
import jax.numpy as jnp
from jax import lax
from jax.experimental import pallas as pl
from jax.experimental.pallas import tpu as pltpu
from jax.sharding import PartitionSpec as P

MESH = pl.DeviceIdType.MESH
F32 = jnp.float32
BF16 = jnp.bfloat16
FEAT = 128
WIDE = 256
HUBS = 16
LOW = 256
CHUNK = 2048
PIECES = ((4, 3, 5, 2), (6, 1, 7, 0))


def dot_nn(a, b):
    return jnp.dot(a, b, preferred_element_type=F32)


def dot_nt(a, b):
    return lax.dot_general(a, b, (((1,), (1,)), ((), ())), preferred_element_type=F32)


def one_hot(count, row):
    places = lax.broadcasted_iota(jnp.int32, (count, row.shape[1]), 0)
    return (places == row).astype(F32).astype(BF16)


def picks(row, value):
    return (row == value).astype(F32).astype(BF16)


def long_row(ref, start, rows):
    return jnp.concatenate([ref[pl.ds(start + j, 1), :] for j in range(rows)], axis=1)


def await_bytes(ref, sem):
    pltpu.make_async_copy(ref, ref, sem).wait()


def layer_rows(x, mean, upstream, self_weight, mean_weight, bias):
    pre = dot_nn(x, self_weight) + dot_nn(mean, mean_weight) + bias
    sig = jax.nn.sigmoid(pre)
    act = (pre * sig).astype(BF16)
    grad = (upstream.astype(F32) * sig * (1.0 + pre * (1.0 - sig))).astype(BF16)
    return act, grad


def kernel(
    count_ref, feat, cot, w_self, w_mean, bias, src, tgt, rows_in,
    act, fgrad, self_grad, mean_grad, bias_grad,
    ohs, oht, gath, high, xt4, rl, cnt, acc, sums, nmean, pgrad, mrt4, own,
    out_slots, in_slots, back_out, back_in,
    tal_out, tal_in, cnt_out, cnt_in, hub_out, hub_in, hubs_out, hubs_in,
    w1_out, w1_in, b1_out, b1_in, w2_out, w2_in, b2_out, b2_in, w3_out, w3_in, small,
    send_sem, recv_sem, slot_sem, back_sem,
):
    grp = lax.axis_index("grp")
    blk = lax.axis_index("blk")
    chip = lax.div(grp, 2)
    core = lax.rem(grp, 2)
    sibling = grp + 1 - 2 * core
    n_grp, n_blk = 16, 64
    blocks = tgt.shape[0]
    per = CHUNK // 128
    chunks = blocks // per

    barrier = pltpu.get_barrier_semaphore()

    def greet(axis, me, n):
        def body(i, carry):
            pl.semaphore_signal(
                barrier, inc=1, device_id={axis: lax.rem(me + i, n)}, device_id_type=MESH
            )
            return carry

        lax.fori_loop(1, n, body, 0)

    greet("blk", blk, n_blk)
    greet("grp", grp, n_grp)

    def send(axis, peer, source, target, which, arrive):
        pltpu.make_async_remote_copy(
            src_ref=source, dst_ref=target, send_sem=send_sem.at[which], recv_sem=arrive,
            device_id={axis: peer}, device_id_type=MESH,
        ).start()

    def send_all(axis, source, target, which):
        me, n = (blk, n_blk) if axis == "blk" else (grp, n_grp)

        def body(i, carry):
            peer = lax.rem(me + i, n)
            send(axis, peer, source(peer), target.at[me], which, recv_sem.at[which])
            return carry

        lax.fori_loop(1, n, body, 0)

    def arrived(target, which):
        n = target.shape[0]
        await_bytes(target.at[pl.ds(0, n - 1)], recv_sem.at[which])

    eye_small = (
        lax.broadcasted_iota(jnp.int32, (FEAT, FEAT), 0)
        == lax.broadcasted_iota(jnp.int32, (FEAT, FEAT), 1)
    ).astype(F32).astype(BF16)
    eye_low = (
        lax.broadcasted_iota(jnp.int32, (LOW, LOW), 0)
        == lax.broadcasted_iota(jnp.int32, (LOW, LOW), 1)
    ).astype(F32).astype(BF16)

    live = lax.broadcasted_iota(jnp.int32, (blocks, 128), 0) < count_ref[0, 0]
    high[...] = jnp.where(live, lax.shift_right_logical(tgt[...], 8), 99)
    for s in range(4):
        xt4[s * FEAT:(s + 1) * FEAT, :] = dot_nt(
            eye_small, feat[s * LOW:(s + 1) * LOW, :]
        ).astype(BF16)

    cnt[...] = jnp.zeros_like(cnt)

    def take_sources(c, carry):
        source = long_row(src, c * per, per)
        ohs[c] = one_hot(LOW, source & 255)
        oht[c] = one_hot(LOW, long_row(tgt, c * per, per) & 255)
        part = lax.shift_right_logical(source, 8)
        total = jnp.zeros((FEAT, CHUNK), F32)
        for s in range(4):
            total = jnp.where(
                part == s, dot_nn(xt4[s * FEAT:(s + 1) * FEAT, :], ohs[c]), total
            )
        gath[c] = total.astype(BF16)
        cnt[...] += dot_nt(one_hot(16, long_row(high, c * per, per)), oht[c])
        return carry

    lax.fori_loop(0, chunks, take_sources, 0)

    for p in range(n_grp):
        tal_out[p] = (
            cnt[p // 2:p // 2 + 1, (p % 2) * 128:(p % 2) * 128 + 128].astype(BF16).astype(F32)
        )
    cnt_out[...] = jnp.concatenate(
        [cnt[8 + r // 2:9 + r // 2, (r % 2) * 128:(r % 2) * 128 + 128] for r in range(8)], axis=0
    )
    pl.semaphore_wait(barrier, n_blk + n_grp - 2)
    send_all("grp", lambda peer: tal_out.at[peer], tal_in, 0)
    send_all("blk", lambda peer: cnt_out, cnt_in, 1)
    tal_in[grp] = tal_out[grp]
    cnt_in[blk] = cnt_out[...]

    def add_targets(parts):
        acc[...] = jnp.zeros_like(acc)

        def body(c, carry):
            row = long_row(high, c * per, per)
            gathered = gath[c]
            acc[...] += dot_nt(
                jnp.concatenate([gathered * picks(row, t) for t in parts], axis=0), oht[c]
            )
            return carry

        lax.fori_loop(0, chunks, body, 0)

    def slot_piece(offsets):
        towards = [lax.rem(chip + d, 8) for d in offsets]
        add_targets(towards)
        for k, (d, z) in enumerate(zip(offsets, towards)):
            for j in range(2):
                out_slots[2 * z + j] = acc[
                    k * FEAT:(k + 1) * FEAT, j * 128:(j + 1) * 128
                ].astype(BF16)
            for j in range(2):
                if d:
                    peer = 2 * z + j
                elif j:
                    continue
                else:
                    peer = sibling
                send("grp", peer, out_slots.at[peer], in_slots.at[grp], 2, slot_sem.at[d])

    slot_piece(PIECES[0])
    add_targets(range(8, 12))
    for t in range(4):
        turned = dot_nt(eye_low, acc[t * FEAT:(t + 1) * FEAT, :].astype(BF16)).astype(BF16)
        hub_out[t * 16:(t + 1) * 16] = turned.reshape(16, HUBS, FEAT)
    send_all("blk", lambda peer: hub_out.at[peer], hub_in, 3)
    hub_in[blk] = hub_out[blk]
    slot_piece(PIECES[1])
    in_slots[grp] = out_slots[grp]

    for z in range(8):
        rl[z] = one_hot(LOW, long_row(rows_in, 2 * z, 2) & 255)
    arrived(tal_in, 0)
    degree_column = jnp.zeros((LOW, 16), F32)
    degree_row = jnp.zeros((16, LOW), F32)
    for z in range(8):
        place = lax.shift_right_logical(long_row(rows_in, 2 * z, 2), 8)
        tally = jnp.concatenate([tal_in[2 * z], tal_in[2 * z + 1]], axis=1)
        kinds = lax.broadcasted_iota(jnp.int32, (16, LOW), 0)
        marked = jnp.where(kinds == place, tally, 0.0).astype(BF16)
        degree_column += dot_nt(rl[z], marked)
        degree_row += dot_nt(marked, rl[z])
    over_column = 1.0 / jnp.maximum(degree_column, 1.0)
    over_row = 1.0 / jnp.maximum(degree_row, 1.0)

    def from_offset(buffer, sems, d):
        z = lax.rem(chip + 8 - d, 8)
        if d:
            await_bytes(buffer.at[pl.ds(2 * z, 2)], sems.at[d])
        else:
            await_bytes(buffer.at[sibling], sems.at[d])
        return z

    order = PIECES[0] + PIECES[1]
    sums[...] = jnp.zeros_like(sums)
    for d in order:
        z = from_offset(in_slots, slot_sem, d)
        place = lax.shift_right_logical(long_row(rows_in, 2 * z, 2), 8)
        block = jnp.concatenate([in_slots[2 * z], in_slots[2 * z + 1]], axis=1)
        spread = jnp.concatenate([block * picks(place, h) for h in range(4)], axis=0)
        sums[...] += dot_nt(rl[z], spread)

    for h in range(4):
        here = slice(h * LOW, (h + 1) * LOW)
        mean = (sums[:, h * FEAT:(h + 1) * FEAT] * over_column[:, h:h + 1]).astype(BF16)
        nmean[here, :] = mean
        a, g = layer_rows(feat[here, :], mean, cot[here, :], w_self[...], w_mean[...], bias[...])
        act[here, :] = a
        pgrad[here, :] = g
        mrt4[h * FEAT:(h + 1) * FEAT, :] = (
            dot_nt(w_mean[...], g) * over_row[h:h + 1, :]
        ).astype(BF16)

    for d in order:
        z = lax.rem(chip + d, 8)
        place = lax.shift_right_logical(long_row(rows_in, 2 * z, 2), 8)
        every = dot_nn(mrt4[...], rl[z])
        taken = every[:FEAT]
        for h in range(1, 4):
            taken = jnp.where(place == h, every[h * FEAT:(h + 1) * FEAT], taken)
        taken = taken.astype(BF16)
        for j in range(2):
            back_out[2 * z + j] = taken[:, j * 128:(j + 1) * 128]
        for j in range(2):
            if d:
                peer = 2 * z + j
            elif j:
                continue
            else:
                peer = sibling
            send("grp", peer, back_out.at[peer], back_in.at[grp], 4, back_sem.at[d])
    back_in[grp] = back_out[grp]

    first = 4 * LOW - HUBS
    arrived(cnt_in, 1)
    small[...] = jnp.sum(cnt_in[...], axis=0)
    hub_counts = small[pl.ds(lax.div(blk, 8), 1), :]
    lanes = lax.broadcasted_iota(jnp.int32, (HUBS, 128), 1)
    mine = lanes == lax.broadcasted_iota(jnp.int32, (HUBS, 128), 0) + lax.rem(blk, 8) * HUBS
    hub_degree = jnp.sum(jnp.where(mine, hub_counts, 0.0), axis=1, keepdims=True)
    over_hub = 1.0 / jnp.maximum(hub_degree, 1.0)
    arrived(hub_in, 3)
    hub_mean = (jnp.sum(hub_in[...].astype(F32), axis=0) * over_hub).astype(BF16)
    nmean[first:, :] = hub_mean
    a, g = layer_rows(
        feat[first:, :], hub_mean, cot[first:, :], w_self[...], w_mean[...], bias[...]
    )
    act[first:, :] = a
    pgrad[first:, :] = g
    hubs_out[...] = (dot_nt(g, w_mean[...]) * over_hub).astype(BF16)
    send_all("blk", lambda peer: hubs_out, hubs_in, 5)
    hubs_in[blk] = hubs_out[...]

    self_part = jnp.zeros((FEAT, WIDE), F32)
    mean_part = jnp.zeros((FEAT, WIDE), F32)
    bias_part = jnp.zeros((1, WIDE), F32)
    for h in range(4):
        here = slice(h * LOW, (h + 1) * LOW)
        g = pgrad[here, :]
        self_part += dot_nn(xt4[h * FEAT:(h + 1) * FEAT, :], g)
        mean_part += dot_nn(dot_nt(eye_small, nmean[here, :]).astype(BF16), g)
        bias_part += jnp.sum(g.astype(F32), axis=0, keepdims=True)
    for k, part in enumerate((self_part, mean_part)):
        for j in range(2):
            w1_out[(2 * k + j) * 16:(2 * k + j + 1) * 16] = (
                part[:, j * 128:(j + 1) * 128].reshape(16, 8, 128)
            )
    b1_out[...] = bias_part
    send_all("blk", lambda peer: w1_out.at[peer], w1_in, 6)
    send_all("blk", lambda peer: b1_out, b1_in, 7)
    w1_in[blk] = w1_out[blk]
    b1_in[blk] = b1_out[...]

    for h in range(4):
        here = slice(h * LOW, (h + 1) * LOW)
        own[here, :] = dot_nt(pgrad[here, :], w_self[...])

    arrived(w1_in, 6)
    arrived(b1_in, 7)
    w2_out[...] = jnp.sum(w1_in[...], axis=0)
    b2_out[...] = jnp.sum(b1_in[...], axis=0)
    send_all("grp", lambda peer: w2_out, w2_in, 8)
    send_all("grp", lambda peer: b2_out, b2_in, 9)
    w2_in[grp] = w2_out[...]
    b2_in[grp] = b2_out[...]

    def take_targets(table, part, fresh):
        def body(c, carry):
            row = long_row(high, c * per, per)
            before = jnp.zeros((FEAT, CHUNK), F32) if fresh else gath[c].astype(F32)
            for t, block in zip(part, table):
                before = jnp.where(row == t, dot_nn(block, oht[c]), before)
            gath[c] = before.astype(BF16)
            return carry

        lax.fori_loop(0, chunks, body, 0)

    arrived(hubs_in, 5)
    take_targets(
        [
            dot_nt(eye_small, hubs_in[t * 16:(t + 1) * 16].reshape(LOW, FEAT)).astype(BF16)
            for t in range(4)
        ],
        range(8, 12),
        True,
    )

    def back_piece(offsets):
        places = [from_offset(back_in, back_sem, d) for d in offsets]
        take_targets(
            [jnp.concatenate([back_in[2 * z], back_in[2 * z + 1]], axis=1) for z in places],
            places,
            False,
        )

    back_piece(order[:4])
    arrived(w2_in, 8)
    arrived(b2_in, 9)
    w3_out[...] = jnp.sum(w2_in[...], axis=0)
    bias_grad[...] = jnp.sum(b2_in[...], axis=0)
    send_all("blk", lambda peer: w3_out, w3_in, 10)
    w3_in[blk] = w3_out[...]
    back_piece(order[4:])

    sums[...] = jnp.zeros_like(sums)

    def add_sources(c, carry):
        part = lax.shift_right_logical(long_row(src, c * per, per), 8)
        gathered = gath[c]
        sums[...] += dot_nt(
            ohs[c], jnp.concatenate([gathered * picks(part, s) for s in range(4)], axis=0)
        )
        return carry

    lax.fori_loop(0, chunks, add_sources, 0)
    for s in range(4):
        here = slice(s * LOW, (s + 1) * LOW)
        fgrad[here, :] = (own[here, :] + sums[:, s * FEAT:(s + 1) * FEAT]).astype(BF16)

    arrived(w3_in, 10)
    for k, grad in enumerate((self_grad, mean_grad)):
        for j in range(2):
            grad[:, j * 128:(j + 1) * 128] = (
                w3_in[(2 * k + j) * 16:(2 * k + j + 1) * 16].reshape(FEAT, 128)
            )

    sent = ((tal_in, 0), (cnt_in, 1), (in_slots, 2), (hub_in, 3), (back_in, 4), (hubs_in, 5),
            (w1_in, 6), (b1_in, 7), (w2_in, 8), (b2_in, 9), (w3_in, 10))
    for buffer, which in sent:
        await_bytes(buffer.at[pl.ds(0, buffer.shape[0] - 1)], send_sem.at[which])


def local(
    features, cotangent, self_weight, mean_weight, bias_term,
    edge_source, edge_target, block_counts, receive_rows,
):
    vertices = features.shape[0]
    blocks = edge_source.shape[2]
    chunks = blocks * 128 // CHUNK
    whole = pl.BlockSpec(memory_space=pltpu.VMEM)
    shape = jax.ShapeDtypeStruct
    act, fgrad, self_grad, mean_grad, bias_grad = pl.pallas_call(
        kernel,
        out_shape=(
            shape((vertices, WIDE), BF16),
            shape((vertices, FEAT), BF16),
            shape((FEAT, WIDE), F32),
            shape((FEAT, WIDE), F32),
            shape((1, WIDE), F32),
        ),
        in_specs=[pl.BlockSpec(memory_space=pltpu.SMEM)] + [whole] * 8,
        out_specs=[whole] * 5,
        scratch_shapes=[
            pltpu.VMEM((chunks, LOW, CHUNK), BF16),
            pltpu.VMEM((chunks, LOW, CHUNK), BF16),
            pltpu.VMEM((chunks, FEAT, CHUNK), BF16),
            pltpu.VMEM((blocks, 128), jnp.int32),
            pltpu.VMEM((4 * FEAT, LOW), BF16),
            pltpu.VMEM((8, LOW, 256), BF16),
            pltpu.VMEM((16, LOW), F32),
            pltpu.VMEM((4 * FEAT, LOW), F32),
            pltpu.VMEM((LOW, 4 * FEAT), F32),
            pltpu.VMEM((vertices, FEAT), BF16),
            pltpu.VMEM((vertices, WIDE), BF16),
            pltpu.VMEM((4 * FEAT, LOW), BF16),
            pltpu.VMEM((vertices, FEAT), F32),
            pltpu.VMEM((16, FEAT, 128), BF16),
            pltpu.VMEM((16, FEAT, 128), BF16),
            pltpu.VMEM((16, FEAT, 128), BF16),
            pltpu.VMEM((16, FEAT, 128), BF16),
            pltpu.VMEM((16, 1, 128), F32),
            pltpu.VMEM((16, 1, 128), F32),
            pltpu.VMEM((8, 128), F32),
            pltpu.VMEM((64, 8, 128), F32),
            pltpu.VMEM((64, HUBS, FEAT), BF16),
            pltpu.VMEM((64, HUBS, FEAT), BF16),
            pltpu.VMEM((HUBS, FEAT), BF16),
            pltpu.VMEM((64, HUBS, FEAT), BF16),
            pltpu.VMEM((64, 8, 128), F32),
            pltpu.VMEM((64, 8, 128), F32),
            pltpu.VMEM((1, WIDE), F32),
            pltpu.VMEM((64, 1, WIDE), F32),
            pltpu.VMEM((8, 128), F32),
            pltpu.VMEM((16, 8, 128), F32),
            pltpu.VMEM((1, WIDE), F32),
            pltpu.VMEM((16, 1, WIDE), F32),
            pltpu.VMEM((8, 128), F32),
            pltpu.VMEM((64, 8, 128), F32),
            pltpu.VMEM((8, 128), F32),
            pltpu.SemaphoreType.DMA((11,)),
            pltpu.SemaphoreType.DMA((11,)),
            pltpu.SemaphoreType.DMA((8,)),
            pltpu.SemaphoreType.DMA((8,)),
        ],
        compiler_params=pltpu.CompilerParams(
            collective_id=0, has_side_effects=True, vmem_limit_bytes=50 * 1024 * 1024
        ),
        name="sage_layer",
    )(
        block_counts,
        features,
        cotangent,
        self_weight,
        mean_weight,
        bias_term.reshape(1, WIDE),
        edge_source.reshape(blocks, 128),
        edge_target.reshape(blocks, 128),
        receive_rows.reshape(16, 128),
    )
    return act, fgrad, self_grad, mean_grad, bias_grad.reshape(WIDE)


def solution(mesh):
    placed = (
        P(("grp", "blk"), None),
        P(("grp", "blk"), None),
        P(),
        P(),
        P(),
        P("grp", "blk", None, None),
        P("grp", "blk", None, None),
        P("grp", "blk"),
        P("grp", "blk", None, None),
    )
    return jax.shard_map(
        local,
        mesh=mesh,
        in_specs=placed,
        out_specs=(P(("grp", "blk"), None), P(("grp", "blk"), None), P(), P(), P()),
        check_vma=False,
    )
```

```python
import jax
import jax.numpy as jnp
from jax import lax
from jax.experimental import pallas as pl
from jax.experimental.pallas import tpu as pltpu
from jax.sharding import PartitionSpec as P

MESH = pl.DeviceIdType.MESH
F32 = jnp.float32
BF16 = jnp.bfloat16
FEAT = 128
WIDE = 256
HUBS = 16
LOW = 256
CHUNK = 2048
PIECES = ((4, 3, 5, 2), (6, 1, 7, 0))


def dot_nn(a, b):
    return jnp.dot(a, b, preferred_element_type=F32)


def dot_nt(a, b):
    return lax.dot_general(a, b, (((1,), (1,)), ((), ())), preferred_element_type=F32)


def one_hot(count, row):
    places = lax.broadcasted_iota(jnp.int32, (count, row.shape[1]), 0)
    return (places == row).astype(F32).astype(BF16)


def picks(row, value):
    return (row == value).astype(F32).astype(BF16)


def long_row(ref, start, rows):
    return jnp.concatenate([ref[pl.ds(start + j, 1), :] for j in range(rows)], axis=1)


def await_bytes(ref, sem):
    pltpu.make_async_copy(ref, ref, sem).wait()


def layer_rows(x, mean, upstream, self_weight, mean_weight, bias):
    pre = dot_nn(x, self_weight) + dot_nn(mean, mean_weight) + bias
    sig = jax.nn.sigmoid(pre)
    act = (pre * sig).astype(BF16)
    grad = (upstream.astype(F32) * sig * (1.0 + pre * (1.0 - sig))).astype(BF16)
    return act, grad


def kernel(
    count_ref, feat_hbm, cot_hbm, w_self_hbm, w_mean_hbm, bias_hbm, src_hbm, tgt_hbm, rows_hbm,
    act_hbm, fgrad_hbm, self_grad, mean_grad, bias_grad,
    feat, cot, w_self, w_mean, bias, src, tgt, rows_in, act, fgrad,
    ohs, oht, gath, high, xt4, rl, cnt, acc, sums, nmean, pgrad, mrt4, own,
    out_slots, in_slots, back_out, back_in,
    tal_out, tal_in, cnt_out, cnt_in, hub_out, hub_in, hubs_out, hubs_in,
    w1_out, w1_in, b1_out, b1_in, w2_out, w2_in, b2_out, b2_in, w3_out, w3_in, small, relay_in,
    send_sem, recv_sem, slot_sem, back_sem, relay_sem, load_sem, store_sem,
):
    loads = [
        pltpu.make_async_copy(source, target, load_sem.at[k])
        for k, (source, target) in enumerate((
            (tgt_hbm, tgt), (src_hbm, src), (feat_hbm, feat), (rows_hbm, rows_in),
            (w_mean_hbm, w_mean), (w_self_hbm, w_self), (bias_hbm, bias), (cot_hbm, cot),
        ))
    ]
    for copy in loads:
        copy.start()
    grp = lax.axis_index("grp")
    blk = lax.axis_index("blk")
    chip = lax.div(grp, 2)
    core = lax.rem(grp, 2)
    sibling = grp + 1 - 2 * core
    n_grp, n_blk = 16, 64
    blocks = tgt.shape[0]
    per = CHUNK // 128
    chunks = blocks // per

    barrier = pltpu.get_barrier_semaphore()

    def greet(axis, me, n):
        def body(i, carry):
            pl.semaphore_signal(
                barrier, inc=1, device_id={axis: lax.rem(me + i, n)}, device_id_type=MESH
            )
            return carry

        lax.fori_loop(1, n, body, 0)

    greet("blk", blk, n_blk)
    greet("grp", grp, n_grp)

    def send(axis, peer, source, target, which, arrive):
        pltpu.make_async_remote_copy(
            src_ref=source, dst_ref=target, send_sem=send_sem.at[which], recv_sem=arrive,
            device_id={axis: peer}, device_id_type=MESH,
        ).start()

    def send_all(axis, source, target, which):
        me, n = (blk, n_blk) if axis == "blk" else (grp, n_grp)

        def body(i, carry):
            peer = lax.rem(me + i, n)
            send(axis, peer, source(peer), target.at[me], which, recv_sem.at[which])
            return carry

        lax.fori_loop(1, n, body, 0)

    def arrived(target, which):
        n = target.shape[0]
        await_bytes(target.at[pl.ds(0, n - 1)], recv_sem.at[which])

    eye_small = (
        lax.broadcasted_iota(jnp.int32, (FEAT, FEAT), 0)
        == lax.broadcasted_iota(jnp.int32, (FEAT, FEAT), 1)
    ).astype(F32).astype(BF16)
    eye_low = (
        lax.broadcasted_iota(jnp.int32, (LOW, LOW), 0)
        == lax.broadcasted_iota(jnp.int32, (LOW, LOW), 1)
    ).astype(F32).astype(BF16)

    for copy in loads[:3]:
        copy.wait()

    live = lax.broadcasted_iota(jnp.int32, (blocks, 128), 0) < count_ref[0, 0]
    high[...] = jnp.where(live, lax.shift_right_logical(tgt[...], 8), 99)
    for s in range(4):
        xt4[s * FEAT:(s + 1) * FEAT, :] = dot_nt(
            eye_small, feat[s * LOW:(s + 1) * LOW, :]
        ).astype(BF16)

    cnt[...] = jnp.zeros_like(cnt)

    def take_sources(c, carry):
        source = long_row(src, c * per, per)
        ohs[c] = one_hot(LOW, source & 255)
        oht[c] = one_hot(LOW, long_row(tgt, c * per, per) & 255)
        part = lax.shift_right_logical(source, 8)
        total = jnp.zeros((FEAT, CHUNK), F32)
        for s in range(4):
            total = jnp.where(
                part == s, dot_nn(xt4[s * FEAT:(s + 1) * FEAT, :], ohs[c]), total
            )
        gath[c] = total.astype(BF16)
        cnt[...] += dot_nt(one_hot(16, long_row(high, c * per, per)), oht[c])
        return carry

    lax.fori_loop(0, chunks, take_sources, 0)

    for p in range(n_grp):
        tal_out[p] = (
            cnt[p // 2:p // 2 + 1, (p % 2) * 128:(p % 2) * 128 + 128].astype(BF16).astype(F32)
        )
    cnt_out[...] = jnp.concatenate(
        [cnt[8 + r // 2:9 + r // 2, (r % 2) * 128:(r % 2) * 128 + 128] for r in range(8)], axis=0
    )
    pl.semaphore_wait(barrier, n_blk + n_grp - 2)
    send_all("grp", lambda peer: tal_out.at[peer], tal_in, 0)
    send_all("blk", lambda peer: cnt_out, cnt_in, 1)
    tal_in[grp] = tal_out[grp]
    cnt_in[blk] = cnt_out[...]

    def add_targets(parts):
        size = len(parts) * FEAT
        acc[:size, :] = jnp.zeros((size, LOW), F32)

        def body(c, carry):
            row = long_row(high, c * per, per)
            gathered = gath[c]
            acc[:size, :] += dot_nt(
                jnp.concatenate([gathered * picks(row, t) for t in parts], axis=0), oht[c]
            )
            return carry

        lax.fori_loop(0, chunks, body, 0)

    before, across = lax.rem(chip + 7, 8), lax.rem(chip + 5, 8)
    after = lax.rem(chip + 1, 8)

    def send_blocks(d, z, out, into, which, sems):
        if d == 0:
            send("grp", sibling, out.at[sibling], into.at[grp], which, sems.at[d])
        elif d == 4:
            straight = 2 * z + core
            send("grp", straight, out.at[straight], into.at[grp], which, sems.at[d])
            relay = relay_in.at[which // 4]
            send(
                "grp", 2 * before + core, out.at[2 * z + 1 - core], relay,
                which, relay_sem.at[which // 4],
            )
        else:
            for j in range(2):
                send("grp", 2 * z + j, out.at[2 * z + j], into.at[grp], which, sems.at[d])

    def hand_over(into, which, sems):
        relay = relay_in.at[which // 4]
        await_bytes(relay, relay_sem.at[which // 4])
        send(
            "grp", 2 * across + 1 - core, relay, into.at[2 * after + core],
            11 + which // 4, sems.at[4],
        )

    def slot_piece(offsets):
        towards = [lax.rem(chip + d, 8) for d in offsets]
        add_targets(towards)
        for k, (d, z) in enumerate(zip(offsets, towards)):
            for j in range(2):
                out_slots[2 * z + j] = acc[
                    k * FEAT:(k + 1) * FEAT, j * 128:(j + 1) * 128
                ].astype(BF16)
            send_blocks(d, z, out_slots, in_slots, 2, slot_sem)

    slot_piece(PIECES[0])
    add_targets(range(8, 12))
    for t in range(4):
        turned = dot_nt(eye_low, acc[t * FEAT:(t + 1) * FEAT, :].astype(BF16)).astype(BF16)
        hub_out[t * 16:(t + 1) * 16] = turned.reshape(16, HUBS, FEAT)
    send_all("blk", lambda peer: hub_out.at[peer], hub_in, 3)
    hub_in[blk] = hub_out[blk]
    hand_over(in_slots, 2, slot_sem)
    slot_piece(PIECES[1])
    in_slots[grp] = out_slots[grp]

    for copy in loads[3:]:
        copy.wait()

    for z in range(8):
        rl[z] = one_hot(LOW, long_row(rows_in, 2 * z, 2) & 255)
    arrived(tal_in, 0)
    degree_column = jnp.zeros((LOW, 16), F32)
    degree_row = jnp.zeros((16, LOW), F32)
    for z in range(8):
        place = lax.shift_right_logical(long_row(rows_in, 2 * z, 2), 8)
        tally = jnp.concatenate([tal_in[2 * z], tal_in[2 * z + 1]], axis=1)
        kinds = lax.broadcasted_iota(jnp.int32, (16, LOW), 0)
        marked = jnp.where(kinds == place, tally, 0.0).astype(BF16)
        degree_column += dot_nt(rl[z], marked)
        degree_row += dot_nt(marked, rl[z])
    over_column = 1.0 / jnp.maximum(degree_column, 1.0)
    over_row = 1.0 / jnp.maximum(degree_row, 1.0)

    def from_offset(buffer, sems, d):
        z = lax.rem(chip + 8 - d, 8)
        if d:
            await_bytes(buffer.at[pl.ds(2 * z, 2)], sems.at[d])
        else:
            await_bytes(buffer.at[sibling], sems.at[d])
        return z

    order = PIECES[0] + PIECES[1]
    sums[...] = jnp.zeros_like(sums)
    for d in order[1:] + order[:1]:
        z = from_offset(in_slots, slot_sem, d)
        place = lax.shift_right_logical(long_row(rows_in, 2 * z, 2), 8)
        block = jnp.concatenate([in_slots[2 * z], in_slots[2 * z + 1]], axis=1)
        spread = jnp.concatenate([block * picks(place, h) for h in range(4)], axis=0)
        sums[...] += dot_nt(rl[z], spread)

    for h in range(4):
        here = slice(h * LOW, (h + 1) * LOW)
        mean = (sums[:, h * FEAT:(h + 1) * FEAT] * over_column[:, h:h + 1]).astype(BF16)
        nmean[here, :] = mean
        a, g = layer_rows(feat[here, :], mean, cot[here, :], w_self[...], w_mean[...], bias[...])
        act[here, :] = a
        pgrad[here, :] = g
        mrt4[h * FEAT:(h + 1) * FEAT, :] = (
            dot_nt(w_mean[...], g) * over_row[h:h + 1, :]
        ).astype(BF16)

    for d in order:
        z = lax.rem(chip + d, 8)
        place = lax.shift_right_logical(long_row(rows_in, 2 * z, 2), 8)
        every = dot_nn(mrt4[...], rl[z])
        taken = every[:FEAT]
        for h in range(1, 4):
            taken = jnp.where(place == h, every[h * FEAT:(h + 1) * FEAT], taken)
        taken = taken.astype(BF16)
        for j in range(2):
            back_out[2 * z + j] = taken[:, j * 128:(j + 1) * 128]
        send_blocks(d, z, back_out, back_in, 4, back_sem)
    back_in[grp] = back_out[grp]

    first = 4 * LOW - HUBS
    arrived(cnt_in, 1)
    small[...] = jnp.sum(cnt_in[...], axis=0)
    hub_counts = small[pl.ds(lax.div(blk, 8), 1), :]
    lanes = lax.broadcasted_iota(jnp.int32, (HUBS, 128), 1)
    mine = lanes == lax.broadcasted_iota(jnp.int32, (HUBS, 128), 0) + lax.rem(blk, 8) * HUBS
    hub_degree = jnp.sum(jnp.where(mine, hub_counts, 0.0), axis=1, keepdims=True)
    over_hub = 1.0 / jnp.maximum(hub_degree, 1.0)
    arrived(hub_in, 3)
    hub_mean = (jnp.sum(hub_in[...].astype(F32), axis=0) * over_hub).astype(BF16)
    nmean[first:, :] = hub_mean
    a, hub_grad = layer_rows(
        feat[first:, :], hub_mean, cot[first:, :], w_self[...], w_mean[...], bias[...]
    )
    act[first:, :] = a
    pgrad[first:, :] = hub_grad
    act_copy = pltpu.make_async_copy(act, act_hbm, store_sem.at[0])
    act_copy.start()

    self_part = jnp.zeros((FEAT, WIDE), F32)
    mean_part = jnp.zeros((FEAT, WIDE), F32)
    bias_part = jnp.zeros((1, WIDE), F32)
    for h in range(4):
        here = slice(h * LOW, (h + 1) * LOW)
        g = pgrad[here, :]
        self_part += dot_nn(xt4[h * FEAT:(h + 1) * FEAT, :], g)
        mean_part += dot_nn(dot_nt(eye_small, nmean[here, :]).astype(BF16), g)
        bias_part += jnp.sum(g.astype(F32), axis=0, keepdims=True)
    for k, part in enumerate((self_part, mean_part)):
        for j in range(2):
            w1_out[(2 * k + j) * 16:(2 * k + j + 1) * 16] = (
                part[:, j * 128:(j + 1) * 128].reshape(16, 8, 128)
            )
    b1_out[...] = bias_part
    send_all("blk", lambda peer: w1_out.at[peer], w1_in, 6)
    send_all("blk", lambda peer: b1_out, b1_in, 7)
    w1_in[blk] = w1_out[blk]
    b1_in[blk] = b1_out[...]

    hubs_out[...] = (dot_nt(hub_grad, w_mean[...]) * over_hub).astype(BF16)
    send_all("blk", lambda peer: hubs_out, hubs_in, 5)
    hubs_in[blk] = hubs_out[...]
    hand_over(back_in, 4, back_sem)
    for h in range(4):
        here = slice(h * LOW, (h + 1) * LOW)
        own[here, :] = dot_nt(pgrad[here, :], w_self[...])

    arrived(w1_in, 6)
    arrived(b1_in, 7)
    w2_out[...] = jnp.sum(w1_in[...], axis=0)
    b2_out[...] = jnp.sum(b1_in[...], axis=0)
    send_all("grp", lambda peer: w2_out, w2_in, 8)
    send_all("grp", lambda peer: b2_out, b2_in, 9)
    w2_in[grp] = w2_out[...]
    b2_in[grp] = b2_out[...]

    sums[...] = jnp.zeros_like(sums)

    def take_targets(table, part, first_piece):
        def body(c, carry):
            row = long_row(high, c * per, per)
            before = jnp.zeros((FEAT, CHUNK), F32) if first_piece else gath[c].astype(F32)
            for t, block in zip(part, table):
                before = jnp.where(row == t, dot_nn(block, oht[c]), before)
            gathered = before.astype(BF16)
            if first_piece:
                gath[c] = gathered
                return carry
            kind = lax.shift_right_logical(long_row(src, c * per, per), 8)
            sums[...] += dot_nt(
                ohs[c], jnp.concatenate([gathered * picks(kind, s) for s in range(4)], axis=0)
            )
            return carry

        lax.fori_loop(0, chunks, body, 0)

    def back_table(offsets):
        places = [from_offset(back_in, back_sem, d) for d in offsets]
        table = [jnp.concatenate([back_in[2 * z], back_in[2 * z + 1]], axis=1) for z in places]
        return table, places

    take_targets(*back_table(order[1:5]), True)
    arrived(w2_in, 8)
    arrived(b2_in, 9)
    w3_out[...] = jnp.sum(w2_in[...], axis=0)
    bias_grad[...] = jnp.sum(b2_in[...], axis=0)
    send_all("blk", lambda peer: w3_out, w3_in, 10)
    w3_in[blk] = w3_out[...]
    table, places = back_table(order[5:] + order[:1])
    arrived(hubs_in, 5)
    table += [
        dot_nt(eye_small, hubs_in[t * 16:(t + 1) * 16].reshape(LOW, FEAT)).astype(BF16)
        for t in range(4)
    ]
    take_targets(table, places + [8, 9, 10, 11], False)
    for s in range(4):
        here = slice(s * LOW, (s + 1) * LOW)
        fgrad[here, :] = (own[here, :] + sums[:, s * FEAT:(s + 1) * FEAT]).astype(BF16)

    fgrad_copy = pltpu.make_async_copy(fgrad, fgrad_hbm, store_sem.at[1])
    fgrad_copy.start()
    arrived(w3_in, 10)
    for k, grad in enumerate((self_grad, mean_grad)):
        for j in range(2):
            grad[:, j * 128:(j + 1) * 128] = (
                w3_in[(2 * k + j) * 16:(2 * k + j + 1) * 16].reshape(FEAT, 128)
            )

    sent = ((tal_in, 0), (cnt_in, 1), (in_slots, 2), (hub_in, 3), (back_in, 4), (hubs_in, 5),
            (w1_in, 6), (b1_in, 7), (w2_in, 8), (b2_in, 9), (w3_in, 10))
    for buffer, which in sent:
        await_bytes(buffer.at[pl.ds(0, buffer.shape[0] - 1)], send_sem.at[which])
    for k in range(2):
        await_bytes(relay_in.at[k], send_sem.at[11 + k])
    act_copy.wait()
    fgrad_copy.wait()


def hand_on(*refs):
    n = 5
    given, wanted, held, came, left = refs[:n], refs[n:2 * n], refs[2 * n:3 * n], refs[-2], refs[-1]
    loads = [pltpu.make_async_copy(given[k], held[k], came.at[k]) for k in range(n)]
    stores = [pltpu.make_async_copy(held[k], wanted[k], left.at[k]) for k in range(n)]
    for copy in loads:
        copy.start()
    for load, store in zip(loads, stores):
        load.wait()
        store.start()
    for copy in stores:
        copy.wait()


def local(
    features, cotangent, self_weight, mean_weight, bias_term,
    edge_source, edge_target, block_counts, receive_rows,
):
    vertices = features.shape[0]
    blocks = edge_source.shape[2]
    chunks = blocks * 128 // CHUNK
    whole = pl.BlockSpec(memory_space=pltpu.VMEM)
    shape = jax.ShapeDtypeStruct
    far = pl.BlockSpec(memory_space=pl.ANY)
    out_shape = (
        shape((vertices, WIDE), BF16),
        shape((vertices, FEAT), BF16),
        shape((FEAT, WIDE), F32),
        shape((FEAT, WIDE), F32),
        shape((1, WIDE), F32),
    )
    results = pl.pallas_call(
        kernel,
        out_shape=out_shape,
        in_specs=[pl.BlockSpec(memory_space=pltpu.SMEM)] + [pl.BlockSpec(memory_space=pltpu.HBM)] * 8,
        out_specs=[far] * 2 + [whole] * 3,
        scratch_shapes=[
            pltpu.VMEM((vertices, FEAT), BF16),
            pltpu.VMEM((vertices, WIDE), BF16),
            pltpu.VMEM((FEAT, WIDE), BF16),
            pltpu.VMEM((FEAT, WIDE), BF16),
            pltpu.VMEM((1, WIDE), F32),
            pltpu.VMEM((blocks, 128), jnp.int32),
            pltpu.VMEM((blocks, 128), jnp.int32),
            pltpu.VMEM((16, 128), jnp.int32),
            pltpu.VMEM((vertices, WIDE), BF16),
            pltpu.VMEM((vertices, FEAT), BF16),
            pltpu.VMEM((chunks, LOW, CHUNK), BF16),
            pltpu.VMEM((chunks, LOW, CHUNK), BF16),
            pltpu.VMEM((chunks, FEAT, CHUNK), BF16),
            pltpu.VMEM((blocks, 128), jnp.int32),
            pltpu.VMEM((4 * FEAT, LOW), BF16),
            pltpu.VMEM((8, LOW, 256), BF16),
            pltpu.VMEM((16, LOW), F32),
            pltpu.VMEM((4 * FEAT, LOW), F32),
            pltpu.VMEM((LOW, 4 * FEAT), F32),
            pltpu.VMEM((vertices, FEAT), BF16),
            pltpu.VMEM((vertices, WIDE), BF16),
            pltpu.VMEM((4 * FEAT, LOW), BF16),
            pltpu.VMEM((vertices, FEAT), F32),
            pltpu.VMEM((16, FEAT, 128), BF16),
            pltpu.VMEM((16, FEAT, 128), BF16),
            pltpu.VMEM((16, FEAT, 128), BF16),
            pltpu.VMEM((16, FEAT, 128), BF16),
            pltpu.VMEM((16, 1, 128), F32),
            pltpu.VMEM((16, 1, 128), F32),
            pltpu.VMEM((8, 128), F32),
            pltpu.VMEM((64, 8, 128), F32),
            pltpu.VMEM((64, HUBS, FEAT), BF16),
            pltpu.VMEM((64, HUBS, FEAT), BF16),
            pltpu.VMEM((HUBS, FEAT), BF16),
            pltpu.VMEM((64, HUBS, FEAT), BF16),
            pltpu.VMEM((64, 8, 128), F32),
            pltpu.VMEM((64, 8, 128), F32),
            pltpu.VMEM((1, WIDE), F32),
            pltpu.VMEM((64, 1, WIDE), F32),
            pltpu.VMEM((8, 128), F32),
            pltpu.VMEM((16, 8, 128), F32),
            pltpu.VMEM((1, WIDE), F32),
            pltpu.VMEM((16, 1, WIDE), F32),
            pltpu.VMEM((8, 128), F32),
            pltpu.VMEM((64, 8, 128), F32),
            pltpu.VMEM((8, 128), F32),
            pltpu.VMEM((2, FEAT, 128), BF16),
            pltpu.SemaphoreType.DMA((13,)),
            pltpu.SemaphoreType.DMA((11,)),
            pltpu.SemaphoreType.DMA((8,)),
            pltpu.SemaphoreType.DMA((8,)),
            pltpu.SemaphoreType.DMA((2,)),
            pltpu.SemaphoreType.DMA((8,)),
            pltpu.SemaphoreType.DMA((2,)),
        ],
        compiler_params=pltpu.CompilerParams(
            collective_id=0, has_side_effects=True, vmem_limit_bytes=63 * 1024 * 1024
        ),
        name="sage_layer",
    )(
        block_counts,
        features,
        cotangent,
        self_weight,
        mean_weight,
        bias_term.reshape(1, WIDE),
        edge_source.reshape(blocks, 128),
        edge_target.reshape(blocks, 128),
        receive_rows.reshape(16, 128),
    )
    act, fgrad, self_grad, mean_grad, bias_grad = pl.pallas_call(
        hand_on,
        out_shape=out_shape,
        in_specs=[far] * 5,
        out_specs=[far] * 5,
        scratch_shapes=[pltpu.VMEM(one.shape, one.dtype) for one in out_shape]
        + [pltpu.SemaphoreType.DMA((5,))] * 2,
        compiler_params=pltpu.CompilerParams(vmem_limit_bytes=63 * 1024 * 1024),
        name="hand_on",
    )(*results)
    return act, fgrad, self_grad, mean_grad, bias_grad.reshape(WIDE)


def solution(mesh):
    placed = (
        P(("grp", "blk"), None),
        P(("grp", "blk"), None),
        P(),
        P(),
        P(),
        P("grp", "blk", None, None),
        P("grp", "blk", None, None),
        P("grp", "blk"),
        P("grp", "blk", None, None),
    )
    return jax.shard_map(
        local,
        mesh=mesh,
        in_specs=placed,
        out_specs=(P(("grp", "blk"), None), P(("grp", "blk"), None), P(), P(), P()),
        check_vma=False,
    )
```
